256 devices in a mesh: pair: 32 (over z_lo, x, y), virt: 8 (over z_hi, core).
Axes of the slice: x: 4, y: 4, z: 8 (z_hi: 4, z_lo: 2; z = z_hi * 2 + z_lo), core: 2. Of those that a mesh axis runs over, the one named last changes fastest.
Arguments:
- amplitudes: float32 [32, 2048, 2048], P('pair', 'virt'), may hold values from -6 to 6
- integrals: float32 [32, 2048, 2048], P('pair', 'virt'), may hold values from -12 to 12
- operator: float32 [2048, 2048], P('virt'), may hold values from -0.375 to 0.375
- virt_energy: float32 [2048], replicated, may hold values from 0.5 to 2.5
- pair_energy: float32 [32], P('pair'), may hold values from 1 to 3
- block_mask: int32 [16, 16], replicated, may hold values from 0 to 1, as said below
- partner: int32 [32], replicated, may hold values from 0 to 31, as said below
Outputs:
- updated: float32 [32, 2048, 2048], P('pair', 'virt')
The draws below stay inside these ranges and needn't reach their ends.
Inputs may be any that keep to these rules, and one draw needn't show every extreme that they name: `block_mask`: each block row holds 2 to 10 present blocks; some block row holds exactly 10. partner[partner[p]] = p and partner[p] != p for every pair p.
All inputs are finite; a program needn't handle non-finite values.
Results may differ from the reference program's by a relative error of at most 0.0001.
Values sent between devices are 32-bit elements; how exact they have to be, the bound alone decides.
A program may use at most 128 MiB of HBM per device.

```python
import math
import jax
import jax.numpy as jnp
from jax import lax

V = 2048
BLK = 128
ROW_MAX = 10
ITERS = 2
NB = 16
NPAIR = 32


def draw_block_mask(key, part):
    key = jax.random.fold_in(key, 11)
    key_count, key_top, key_order = jax.random.split(key, 3)
    counts = jax.random.randint(key_count, (NB,), 2, ROW_MAX + 1)
    top_row = jax.random.randint(key_top, (), 0, NB)
    counts = jnp.where(jnp.arange(NB) == top_row, ROW_MAX, counts)
    row_keys = jax.random.split(key_order, NB)
    orders = jax.vmap(lambda k: jax.random.permutation(k, NB))(row_keys)
    ranks = jnp.argsort(orders, axis=1)
    return (ranks < counts[:, None]).astype(jnp.int32)


def draw_partner(key, part):
    key = jax.random.fold_in(key, 23)
    order = jax.random.permutation(key, NPAIR).astype(jnp.int32)
    left_side = order[0::2]
    right_side = order[1::2]
    result = jnp.zeros((NPAIR,), jnp.int32)
    result = result.at[left_side].set(right_side)
    result = result.at[right_side].set(left_side)
    return result


def steps_of(key, shape, cuts, least, high):
    level = 1.0
    for position, blocks in cuts:
        draws = jax.random.uniform(jax.random.fold_in(jax.random.fold_in(key, 6), position), (blocks,), jnp.float32, least / len(cuts), high / len(cuts))
        level = level * jnp.repeat(jnp.exp(draws), shape[position] // blocks).reshape((-1,) + (1,) * (len(shape) - 1 - position))
    return level


def normal_values(key, shape, deviation, most, cuts=(), held_as=jnp.bfloat16):
    factor_of = steps_of(key, shape, cuts, -0.22, 0.18) if cuts else 1.0
    entries = jax.random.normal(key, shape, jnp.float32) * deviation * factor_of
    return jnp.minimum(jnp.maximum(entries, -most), most).astype(held_as)


def setup_inputs(seed: int = 0) -> dict:
    splits = jax.random.split(jax.random.key(seed), 8)
    return {
        "amplitudes": normal_values(splits[0], (NPAIR, V, V), 1.0, 6.0, ((0, 32), (1, 8)), jnp.float32),
        "integrals": normal_values(splits[1], (NPAIR, V, V), 2.0, 12.0, ((0, 32), (1, 8)), jnp.float32),
        "operator": normal_values(splits[2], (V, V), (2 * BLK) ** -0.5, 0.375, ((0, 8),), jnp.float32),
        "virt_energy": jnp.clip(jax.random.uniform(splits[3], (V,), jnp.float32, 0.5, 2.5), 0.5, 2.5),
        "pair_energy": jnp.clip(jnp.exp(math.log(3.0) - 1.0986123 * jax.random.uniform(splits[4], (NPAIR,), jnp.float32) ** steps_of(splits[4], (NPAIR,), ((0, 32),), -0.2, 0.2)), 1.0, 3.0),
        "block_mask": draw_block_mask(jax.random.fold_in(splits[7], 71), 0),
        "partner": draw_partner(jax.random.fold_in(splits[7], 71), 0),
    }


def reference(amplitudes, integrals, operator, virt_energy, pair_energy, block_mask, partner):
    mask_values = block_mask.astype(jnp.float32)
    masked = (operator.reshape(NB, BLK, NB, BLK) * mask_values[:, None, :, None]).reshape(V, V)
    denominator = virt_energy[None, :, None] + virt_energy[None, None, :] + pair_energy[:, None, None]
    current = amplitudes
    for sweep in range(ITERS):
        product = jnp.einsum("pac,cb->pab", current, masked, precision=lax.Precision.HIGHEST)
        mirror = jnp.swapaxes(jnp.take(product, partner.astype(jnp.int32), axis=0), 1, 2)
        current = (integrals + product + mirror) / denominator
    return current
```

```python
import jax
import jax.numpy as jnp
from jax import lax
from jax.experimental import pallas as pl
from jax.experimental.pallas import tpu as pltpu
from jax.sharding import PartitionSpec as P

ITERS = 2
MESH = pl.DeviceIdType.MESH


def mirror_kernel(
    partner_ref, turned_in, mirror, spread, turned, out1, in1, out2, in2, ready
):
    pairs, virts = lax.axis_size("pair"), lax.axis_size("virt")
    total = pairs * virts
    p, v = lax.axis_index("pair"), lax.axis_index("virt")
    me = p * virts + v
    barrier = pltpu.get_barrier_semaphore()

    def tell(semaphore, axis, mine, count):
        def one(step, carry):
            pl.semaphore_signal(
                semaphore,
                inc=1,
                device_id={axis: lax.rem(mine + step, count)},
                device_id_type=MESH,
            )
            return carry

        lax.fori_loop(1, count, one, 0)

    tell(barrier, "pair", p, pairs)
    tell(barrier, "virt", v, virts)
    pl.semaphore_wait(barrier, pairs + virts - 2)
    tell(ready, "virt", v, virts)
    pl.semaphore_wait(ready, virts - 1)

    width = turned_in.shape[2]
    place = pl.ds(pl.multiple_of(v * width, width), width)

    def scatter(step, carry):
        target = lax.rem(me + step, total)
        pair, virt = target // virts, lax.rem(target, virts)
        pltpu.make_async_remote_copy(
            src_ref=turned_in.at[virt * pairs + pair],
            dst_ref=spread.at[p, :, place],
            send_sem=out1,
            recv_sem=in1,
            device_id={"pair": pair, "virt": virt},
            device_id_type=MESH,
        ).start()
        return carry

    lax.fori_loop(1, total, scatter, 0)
    pltpu.make_async_copy(
        turned_in.at[v * pairs + p], spread.at[p, :, place], in1
    ).start()
    pltpu.make_async_copy(spread, spread, in1).wait()

    def give(step, carry):
        pair = lax.rem(p + step, pairs)
        turned[pair] = spread[partner_ref[pair]]
        pltpu.make_async_remote_copy(
            src_ref=turned.at[pair],
            dst_ref=mirror.at[p],
            send_sem=out2,
            recv_sem=in2,
            device_id={"pair": pair},
            device_id_type=MESH,
        ).start()
        return carry

    lax.fori_loop(1, pairs, give, 0)
    turned[p] = spread[partner_ref[p]]
    pltpu.make_async_copy(turned.at[p], mirror.at[p], in2).start()
    sent = turned_in.at[pl.ds(0, total - 1)]
    pltpu.make_async_copy(sent, sent, out1).wait()
    pltpu.make_async_copy(mirror, mirror, in2).wait()
    sent = turned.at[pl.ds(0, pairs - 1)]
    pltpu.make_async_copy(sent, sent, out2).wait()


def mirror_of(product, partner):
    rows, width = product.shape
    pairs, virts = lax.axis_size("pair"), lax.axis_size("virt")
    slab = width // (pairs * virts)
    shape = (pairs, slab, width)
    return pl.pallas_call(
        mirror_kernel,
        out_shape=jax.ShapeDtypeStruct(shape, jnp.float32),
        in_specs=[
            pl.BlockSpec(memory_space=pltpu.SMEM),
            pl.BlockSpec(memory_space=pltpu.VMEM),
        ],
        out_specs=pl.BlockSpec(memory_space=pltpu.VMEM),
        scratch_shapes=[pltpu.VMEM(shape, jnp.float32)] * 2
        + [pltpu.SemaphoreType.DMA] * 4
        + [pltpu.SemaphoreType.REGULAR],
        compiler_params=pltpu.CompilerParams(
            collective_id=0, has_side_effects=True, vmem_limit_bytes=24 << 20
        ),
    )(partner, product.T.reshape(pairs * virts, slab, rows)).reshape(rows, width)


def per_device(amplitudes, integrals, operator, virt_energy, pair_energy, block_mask, partner):
    pair_count, row_count, width = amplitudes.shape
    block_count = block_mask.shape[0]
    block_size = width // block_count
    gathered = lax.all_gather(operator, "virt", axis=0, tiled=True)
    mask_values = block_mask.astype(jnp.float32)
    masked = (
        gathered.reshape(block_count, block_size, block_count, block_size)
        * mask_values[:, None, :, None]
    ).reshape(width, width)
    row_start = lax.axis_index("virt") * row_count
    own_energy = lax.dynamic_slice_in_dim(virt_energy, row_start, row_count)
    denominator = own_energy[:, None] + virt_energy[None, :] + pair_energy[0]
    current = amplitudes[0]
    for sweep in range(ITERS):
        product = jnp.dot(current, masked, precision=lax.Precision.HIGH)
        mirror = mirror_of(product, partner)
        current = (integrals[0] + product + mirror) / denominator
    return current[None]


def solution(mesh):
    return jax.shard_map(
        per_device,
        mesh=mesh,
        in_specs=(
            P("pair", "virt", None),
            P("pair", "virt", None),
            P("virt", None),
            P(),
            P("pair"),
            P(),
            P(),
        ),
        out_specs=P("pair", "virt", None),
        check_vma=False,
    )
```

```python
import jax
import jax.numpy as jnp
from jax import lax
from jax.experimental import pallas as pl
from jax.experimental.pallas import tpu as pltpu
from jax.sharding import PartitionSpec as P

ITERS = 2
MESH = pl.DeviceIdType.MESH
PAIRS, VIRTS = 32, 8
TOTAL = PAIRS * VIRTS
WIDTH, ROWS, BLOCK, BLOCKS, SLOTS = 2048, 256, 128, 16, 10
HALVES = 2
SLAB = WIDTH // TOTAL
F32, BF16 = jnp.float32, jnp.bfloat16
JS = (1, 3, 2)
KINDS = 10


def split(value):
    high = value.astype(BF16)
    return high, (value - high.astype(F32)).astype(BF16)


def three_dots(a_high, a_low, b_high, b_low):
    def dot(a, b):
        return jnp.dot(a, b, preferred_element_type=F32)

    return dot(a_high, b_high) + (dot(a_high, b_low) + dot(a_low, b_high))


def kernel(
    partner_ref, slot_ref, flag_ref, column_ref, pair_ref, amp_hbm, int_hbm, op_hbm, own_ref, virt_ref,
    out_ref,
    amp, ints, op0, op1, prod, a_high, a_low, w_high, w_low, *rest,
):
    got = [[[rest[(j * 2 + cc) * 2 + h] for h in range(2)] for cc in range(2)] for j in range(4)]
    rest = rest[16:]
    turned_in, spread, turned, mirror = (
        rest[0:2], (rest[2:4], rest[4:6]), rest[6:8], (rest[8:10], rest[10:12])
    )
    load_sem, gather_out, gather_in, hop_out, hop_in, ready = rest[12:]

    p, v = lax.axis_index("pair"), lax.axis_index("virt")
    z_lo, x, y = p // 16, lax.rem(p // 4, 4), lax.rem(p, 4)
    z_hi, core = v // 2, lax.rem(v, 2)
    op = (op0, op1)
    barrier = pltpu.get_barrier_semaphore()

    loads = [
        pltpu.make_async_copy(
            op_hbm.at[pl.ds(h * BLOCK, BLOCK), pl.ds(c * BLOCK, BLOCK)], op[h].at[c], load_sem.at[h]
        )
        for h in range(2) for c in range(BLOCKS)
    ] + [
        pltpu.make_async_copy(amp_hbm, amp, load_sem.at[2]),
        pltpu.make_async_copy(int_hbm, ints, load_sem.at[3]),
    ]
    for load in loads:
        load.start()

    def tell(semaphore, axis, mine, count):
        def one(step, carry):
            pl.semaphore_signal(
                semaphore, inc=1, device_id={axis: lax.rem(mine + step, count)}, device_id_type=MESH
            )
            return carry

        lax.fori_loop(1, count, one, 0)

    tell(barrier, "pair", p, PAIRS)
    tell(barrier, "virt", v, VIRTS)

    for h in range(2):
        pltpu.make_async_copy(op[h], op[h], load_sem.at[h]).wait()
        def pack(s, carry, h=h):
            block = op[h][column_ref[(v * 2 + h) * SLOTS + s]]
            got[0][0][h][s] = block.reshape(4, 4, 8, BLOCK)
            return carry

        lax.fori_loop(0, SLOTS, pack, 0)

    pl.semaphore_wait(barrier, PAIRS + VIRTS - 2)
    tell(ready, "virt", v, VIRTS)
    pl.semaphore_wait(ready, VIRTS - 1)

    def place(xx, yy, zz, cc):
        return {"pair": (z_lo * 4 + xx) * 4 + yy, "virt": zz * 2 + cc}

    def remote(number, source, target, device):
        return pltpu.make_async_remote_copy(
            src_ref=source, dst_ref=target, send_sem=gather_out.at[number], recv_sem=gather_in.at[number],
            device_id=device, device_id_type=MESH,
        )

    everything = []

    def go(copy):
        copy.start()
        everything.append(copy)
        return copy

    def turn4(value, by):
        return lax.rem(value + (by + 4), 4)

    units = [(j, h) for j in JS for h in range(2)]
    base = {u: i * KINDS for i, u in enumerate(units)}
    core_copy = {}
    for h in range(2):
        mine = got[0][0][h]
        for j in JS:
            go(remote(base[j, h], mine.at[:, x, y], got[j][0][h].at[:, x, y], place(x, y, turn4(z_hi, j), core)))
    for h in range(2):
        core_copy[0, h] = go(
            remote(6 * KINDS + h, got[0][0][h], got[0][1][h], place(x, y, z_hi, 1 - core))
        )

    def along(h, by, first):
        if (h == 0) == first:
            return place(turn4(x, by), y, z_hi, core)
        return place(x, turn4(y, by), z_hi, core)

    def view(unit, a, b, slots=slice(None)):
        j, h = unit
        i, k = (a, b) if h == 0 else (b, a)
        return got[j][0][h].at[slots, i, k]

    low, high = pl.ds(0, SLOTS // 2), pl.ds(SLOTS // 2, SLOTS // 2)
    whole = slice(None)

    def own(h):
        return (x, y) if h == 0 else (y, x)

    def from_z(unit):
        number = base[unit]
        a, b = own(unit[1])
        remote(number, view(unit, a, b), view(unit, a, b), place(x, y, z_hi, core)).wait_recv()
        for kind, by in ((1, 1), (2, -1)):
            go(remote(number + kind, view(unit, a, b), view(unit, a, b), along(unit[1], by, True)))

    def first_forward(unit):
        number = base[unit]
        a, b = own(unit[1])
        for kind, by, part in ((1, 1, low), (2, -1, high)):
            behind = turn4(a, -by)
            block = view(unit, behind, b)
            remote(number + kind, block, block, along(unit[1], by, True)).wait_recv()
            block = view(unit, behind, b, part)
            go(remote(number + kind + 2, block, block, along(unit[1], by, True)))

    def second(unit):
        number = base[unit]
        a, b = own(unit[1])
        for kind, by, part in ((3, 1, low), (4, -1, high)):
            block = view(unit, turn4(a, 2), b, part)
            remote(number + kind, block, block, along(unit[1], by, True)).wait_recv()
        for kind, by in ((5, 1), (6, -1)):
            block = view(unit, whole, b)
            go(remote(number + kind, block, block, along(unit[1], by, False)))

    def second_forward(unit):
        number = base[unit]
        a, b = own(unit[1])
        for kind, by, part in ((5, 1, low), (6, -1, high)):
            behind = turn4(b, -by)
            block = view(unit, whole, behind)
            remote(number + kind, block, block, along(unit[1], by, False)).wait_recv()
            block = view(unit, whole, behind, part)
            go(remote(number + kind + 2, block, block, along(unit[1], by, False)))

    def complete(unit):
        number = base[unit]
        a, b = own(unit[1])
        for kind, by, part in ((7, 1, low), (8, -1, high)):
            block = view(unit, whole, turn4(b, 2), part)
            remote(number + kind, block, block, along(unit[1], by, False)).wait_recv()
        j, h = unit
        core_copy[unit] = go(
            remote(number + 9, got[j][0][h], got[j][1][h], place(x, y, z_hi, 1 - core))
        )

    def row_of(j, cc):
        return turn4(z_hi, -j) * 2 + (core if cc == 0 else 1 - core)

    def split_amplitudes():
        def one(i, carry):
            j = lax.rem(turn4(z_hi, 0) - i // 2 + 4, 4)
            k = j * 2 + lax.rem(i + core, 2)
            for h in range(2):
                value = amp[:, pl.ds(pl.multiple_of(i * ROWS + h * BLOCK, BLOCK), BLOCK)]
                a, b = split(value)
                lanes = pl.ds(pl.multiple_of(k * ROWS + h * BLOCK, BLOCK), BLOCK)
                a_high[:, lanes] = a
                a_low[:, lanes] = b
            return carry

        lax.fori_loop(0, VIRTS, one, 0)

    def expand(j, cc, h):
        k = j * 2 + cc
        source = got[j][cc][h]
        first = (row_of(j, cc) * 2 + h) * BLOCKS
        rows = pl.ds(k * ROWS + h * BLOCK, BLOCK)

        def one(c, carry):
            block = source[slot_ref[first + c]].reshape(BLOCK, BLOCK) * flag_ref[first + c]
            a, b = split(block)
            lanes = pl.ds(pl.multiple_of(c * BLOCK, BLOCK), BLOCK)
            w_high[rows, lanes] = a
            w_low[rows, lanes] = b
            return carry

        lax.fori_loop(0, BLOCKS, one, 0)

    def partial(k):
        rows = pl.ds(k * ROWS, ROWS)

        def one(n, carry):
            lanes = pl.ds(pl.multiple_of(n * 512, 512), 512)
            value = three_dots(a_high[:, rows], a_low[:, rows], w_high[rows, lanes], w_low[rows, lanes])
            if k == 0:
                prod[:, lanes] = value
            else:
                prod[:, lanes] += value
            return carry

        lax.fori_loop(0, WIDTH // 512, one, 0)

    def full():
        def one(n, carry):
            lanes = pl.ds(pl.multiple_of(n * 256, 256), 256)
            prod[:, lanes] = three_dots(a_high[...], a_low[...], w_high[:, lanes], w_low[:, lanes])
            return carry

        lax.fori_loop(0, WIDTH // 256, one, 0)

    def scatter(sweep, h):
        lanes = pl.ds(pl.multiple_of(v * BLOCK, BLOCK), BLOCK)

        def flip(w):
            block = prod[h * BLOCK:(h + 1) * BLOCK, pl.ds(pl.multiple_of(w * ROWS, ROWS), ROWS)]
            turned_in[h][w] = block.T.reshape(PAIRS, SLAB, BLOCK)

        def send(w):
            def one(step, carry):
                pair = lax.rem(p + step, PAIRS)
                pltpu.make_async_remote_copy(
                    src_ref=turned_in[h].at[w, pair], dst_ref=spread[sweep][h].at[p, :, lanes],
                    send_sem=hop_out.at[sweep * 4 + h], recv_sem=hop_in.at[sweep * 4 + h],
                    device_id={"pair": pair, "virt": w}, device_id_type=MESH,
                ).start()
                return carry

            return one

        def others(i, carry):
            w = lax.rem(v + i, VIRTS)
            flip(w)
            lax.fori_loop(0, PAIRS, send(w), 0)
            return carry

        lax.fori_loop(1, VIRTS, others, 0)
        flip(v)
        lax.fori_loop(1, PAIRS, send(v), 0)
        pltpu.make_async_copy(
            turned_in[h].at[v, p], spread[sweep][h].at[p, :, lanes], hop_in.at[sweep * 4 + h]
        ).start()

    def give(sweep, h):
        number = sweep * 4 + h
        pltpu.make_async_copy(spread[sweep][h], spread[sweep][h], hop_in.at[number]).wait()
        number += 2

        def one(step, carry):
            pair = lax.rem(p + step, PAIRS)
            turned[h][pair] = spread[sweep][h][partner_ref[pair]]
            pltpu.make_async_remote_copy(
                src_ref=turned[h].at[pair], dst_ref=mirror[sweep][h].at[p],
                send_sem=hop_out.at[number], recv_sem=hop_in.at[number],
                device_id={"pair": pair}, device_id_type=MESH,
            ).start()
            return carry

        lax.fori_loop(1, PAIRS, one, 0)
        turned[h][p] = spread[sweep][h][partner_ref[p]]
        pltpu.make_async_copy(turned[h].at[p], mirror[sweep][h].at[p], hop_in.at[number]).start()

    def combine(sweep, h):
        number = sweep * 4 + 2 + h
        pltpu.make_async_copy(mirror[sweep][h], mirror[sweep][h], hop_in.at[number]).wait()
        side = own_ref[...]

        def one(i, carry):
            lanes = pl.ds(pl.multiple_of(i * ROWS + h * BLOCK, BLOCK), BLOCK)
            other = mirror[sweep][h][:, :, pl.ds(pl.multiple_of(i * BLOCK, BLOCK), BLOCK)]
            below = side + virt_ref[:1, lanes] + pair_ref[0]
            value = (ints[:, lanes] + prod[:, lanes] + other.reshape(ROWS, BLOCK)) / below
            if sweep == ITERS - 1:
                out_ref[:, lanes] = value
            else:
                j = lax.rem(z_hi - i // 2 + 4, 4)
                k = j * 2 + lax.rem(i + core, 2)
                a, b = split(value)
                lanes = pl.ds(pl.multiple_of(k * ROWS + h * BLOCK, BLOCK), BLOCK)
                a_high[:, lanes] = a
                a_low[:, lanes] = b
            return carry

        lax.fori_loop(0, VIRTS, one, 0)

    def drain(sweep):
        for h in range(HALVES):
            sent = turned_in[h].at[pl.ds(0, VIRTS - 1)]
            pltpu.make_async_copy(sent, sent, hop_out.at[sweep * 4 + h]).wait()
            sent = turned_in[h].at[0, pl.ds(0, PAIRS - 1)]
            pltpu.make_async_copy(sent, sent, hop_out.at[sweep * 4 + h]).wait()
            sent = turned[h].at[pl.ds(0, PAIRS - 1)]
            pltpu.make_async_copy(sent, sent, hop_out.at[sweep * 4 + 2 + h]).wait()

    for unit in units:
        from_z(unit)
    for unit in units:
        first_forward(unit)
    for unit in units:
        second(unit)
    loads[-2].wait()
    split_amplitudes()
    for h in range(2):
        expand(0, 0, h)
    partial(0)
    for unit in units:
        second_forward(unit)
    for h in range(2):
        core_copy[0, h].wait_recv()
        expand(0, 1, h)
    partial(1)
    for j in JS:
        for h in range(2):
            complete((j, h))
            expand(j, 0, h)
        partial(j * 2)
    for j in JS:
        for h in range(2):
            core_copy[j, h].wait_recv()
            expand(j, 1, h)
        partial(j * 2 + 1)
    loads[-1].wait()
    for sweep in range(ITERS):
        if sweep:
            full()
        for h in range(HALVES):
            scatter(sweep, h)
        for h in range(HALVES):
            give(sweep, h)
        for h in range(HALVES):
            combine(sweep, h)
        drain(sweep)
    for copy in everything:
        copy.wait_send()


def per_device(amplitudes, integrals, operator, virt_energy, pair_energy, block_mask, partner):
    v = lax.axis_index("virt")
    own = lax.dynamic_slice_in_dim(virt_energy, v * ROWS, ROWS)
    own = jnp.broadcast_to(own[:, None], (ROWS, BLOCK))
    virt = jnp.broadcast_to(virt_energy[None, :], (8, WIDTH))
    number = jnp.arange(BLOCKS)
    ahead = (number[None, :] < number[:, None]).astype(jnp.int32)
    slot = jnp.sum(block_mask[:, None, :] * ahead[None], axis=2)
    slot = jnp.where(block_mask > 0, slot, 0)
    hit = (slot[:, None, :] == jnp.arange(SLOTS)[None, :, None]) & (block_mask[:, None, :] > 0)
    columns = jnp.sum(jnp.where(hit, number[None, None, :], 0), axis=2)
    smem = pl.BlockSpec(memory_space=pltpu.SMEM)
    vmem = pl.BlockSpec(memory_space=pltpu.VMEM)
    hbm = pl.BlockSpec(memory_space=pl.ANY)
    slab = (PAIRS, SLAB, WIDTH // HALVES)
    result = pl.pallas_call(
        kernel,
        out_shape=jax.ShapeDtypeStruct((ROWS, WIDTH), F32),
        in_specs=[smem] * 5 + [hbm] * 3 + [vmem] * 2,
        out_specs=vmem,
        scratch_shapes=[pltpu.VMEM((ROWS, WIDTH), F32)] * 2
        + [pltpu.VMEM((BLOCKS, BLOCK, BLOCK), F32)] * 2
        + [pltpu.VMEM((ROWS, WIDTH), F32)]
        + [pltpu.VMEM((ROWS, WIDTH), BF16)] * 2
        + [pltpu.VMEM((WIDTH, WIDTH), BF16)] * 2
        + [pltpu.VMEM((SLOTS, 4, 4, 8, BLOCK), F32)] * 16
        + [pltpu.VMEM((VIRTS, PAIRS, SLAB, BLOCK), F32)] * 2
        + [pltpu.VMEM(slab, F32)] * 10
        + [
            pltpu.SemaphoreType.DMA((4,)),
            pltpu.SemaphoreType.DMA((6 * KINDS + 2,)),
            pltpu.SemaphoreType.DMA((6 * KINDS + 2,)),
            pltpu.SemaphoreType.DMA((8,)),
            pltpu.SemaphoreType.DMA((8,)),
            pltpu.SemaphoreType.REGULAR,
        ],
        compiler_params=pltpu.CompilerParams(
            collective_id=0, has_side_effects=True, vmem_limit_bytes=58 << 20
        ),
    )(
        partner, slot.reshape(-1), block_mask.astype(F32).reshape(-1), columns.reshape(-1), pair_energy,
        amplitudes[0], integrals[0], operator, own, virt,
    )
    return result[None]


def solution(mesh):
    return jax.shard_map(
        per_device,
        mesh=mesh,
        in_specs=(
            P("pair", "virt", None),
            P("pair", "virt", None),
            P("virt", None),
            P(),
            P("pair"),
            P(),
            P(),
        ),
        out_specs=P("pair", "virt", None),
        check_vma=False,
    )
```

```python
import jax
import jax.numpy as jnp
from jax import lax
from jax.experimental import pallas as pl
from jax.experimental.pallas import tpu as pltpu
from jax.sharding import PartitionSpec as P

ITERS = 2
MESH = pl.DeviceIdType.MESH
PAIRS, VIRTS = 32, 8
TOTAL = PAIRS * VIRTS
WIDTH, ROWS, BLOCK, BLOCKS, SLOTS = 2048, 256, 128, 16, 10
SLAB = 16
PLANE = PAIRS // 2
F32, BF16 = jnp.float32, jnp.bfloat16
JS = (1, 3, 2)
KINDS = 13
PIECES = {
    (0, 0): (0, 0), (0, 1): (0, 1), (1, 0): (1, 0), (3, 0): (1, 1),
    (1, 1): (2, 0), (3, 1): (2, 1), (2, 0): (3, 0), (2, 1): (3, 1),
}
CHUNKS = 4
ORDER = {piece: c * 2 + plane for piece, (c, plane) in PIECES.items()}


def split(value):
    high = value.astype(BF16)
    return high, (value - high.astype(F32)).astype(BF16)


def three_dots(a_high, a_low, b_high, b_low):
    def dot(a, b):
        return jnp.dot(a, b, preferred_element_type=F32)

    return dot(a_high, b_high) + (dot(a_high, b_low) + dot(a_low, b_high))


def kernel(
    partner_ref, mask_ref, pair_ref, amp_hbm, int_hbm, op_hbm, virt_ref,
    out_ref,
    amp, ints, op0, op1, side, prod0, prod1, a_high, a_low, w_high, w_low, *rest,
):
    got = [[[rest[(j * 2 + cc) * 2 + h] for h in range(2)] for cc in range(2)] for j in range(4)]
    rest = rest[16:]
    turned_in, spread, turned, mirror = (
        rest[0:4], (rest[4:8], rest[8:12]), rest[12:16], (rest[16:20], rest[20:24])
    )
    load_sem, gather_out, gather_in, hop_out, hop_in, ready = rest[24:]

    p, v = lax.axis_index("pair"), lax.axis_index("virt")
    z_lo, x, y = p // 16, lax.rem(p // 4, 4), lax.rem(p, 4)
    z_hi, core = v // 2, lax.rem(v, 2)
    op, prods = (op0, op1), (prod0, prod1)
    barrier = pltpu.get_barrier_semaphore()

    loads = [
        pltpu.make_async_copy(
            op_hbm.at[pl.ds(h * BLOCK, BLOCK), pl.ds(c * BLOCK, BLOCK)], op[h].at[c], load_sem.at[h]
        )
        for h in range(2) for c in range(BLOCKS)
    ] + [
        pltpu.make_async_copy(amp_hbm, amp, load_sem.at[2]),
        pltpu.make_async_copy(int_hbm, ints, load_sem.at[3]),
    ]
    for load in loads:
        load.start()

    def tell(semaphore, axis, mine, count):
        def one(step, carry):
            pl.semaphore_signal(
                semaphore, inc=1, device_id={axis: lax.rem(mine + step, count)}, device_id_type=MESH
            )
            return carry

        lax.fori_loop(1, count, one, 0)

    tell(barrier, "pair", p, PAIRS)
    tell(barrier, "virt", v, VIRTS)

    for h in range(2):
        pltpu.make_async_copy(op[h], op[h], load_sem.at[h]).wait()
        def find(c, carry, h=h):
            count, columns = carry
            here = mask_ref[v * 2 + h, c]
            columns = tuple(
                jnp.where((count == s) & (here > 0), c, column) for s, column in enumerate(columns)
            )
            return count + here, columns

        zero = jnp.int32(0)
        _, columns = lax.fori_loop(0, BLOCKS, find, (zero, (zero,) * SLOTS))
        for s in range(SLOTS):
            got[0][0][h][s] = op[h][columns[s]].reshape(4, 4, 8, BLOCK)

    pl.semaphore_wait(barrier, PAIRS + VIRTS - 2)
    tell(ready, "virt", v, VIRTS)
    pl.semaphore_wait(ready, VIRTS - 1)

    def place(xx, yy, zz, cc):
        return {"pair": (z_lo * 4 + xx) * 4 + yy, "virt": zz * 2 + cc}

    def remote(number, source, target, device):
        return pltpu.make_async_remote_copy(
            src_ref=source, dst_ref=target, send_sem=gather_out.at[number], recv_sem=gather_in.at[number],
            device_id=device, device_id_type=MESH,
        )

    everything = []

    def go(copy):
        copy.start()
        everything.append(copy)
        return copy

    def turn4(value, by):
        return lax.rem(value + (by + 4), 4)

    units = [(j, h) for j in JS for h in range(2)]
    base = {u: i * KINDS for i, u in enumerate(units)}
    core_copy = {}
    for h in range(2):
        mine = got[0][0][h]
        for j in JS:
            go(remote(base[j, h], mine.at[:, x, y], got[j][0][h].at[:, x, y], place(x, y, turn4(z_hi, j), core)))
    for h in range(2):
        core_copy[0, h] = go(
            remote(6 * KINDS + h, got[0][0][h], got[0][1][h], place(x, y, z_hi, 1 - core))
        )

    def along(h, by, first):
        if (h == 0) == first:
            return place(turn4(x, by), y, z_hi, core)
        return place(x, turn4(y, by), z_hi, core)

    def view(unit, a, b, slots=slice(None)):
        j, h = unit
        i, k = (a, b) if h == 0 else (b, a)
        return got[j][0][h].at[slots, i, k]

    low, high = pl.ds(0, SLOTS // 2), pl.ds(SLOTS // 2, SLOTS // 2)
    whole = slice(None)

    def own(h):
        return (x, y) if h == 0 else (y, x)

    def from_z(unit):
        number = base[unit]
        a, b = own(unit[1])
        remote(number, view(unit, a, b), view(unit, a, b), place(x, y, z_hi, core)).wait_recv()
        for kind, by in ((1, 1), (2, -1)):
            go(remote(number + kind, view(unit, a, b), view(unit, a, b), along(unit[1], by, True)))

    def first_forward(unit):
        number = base[unit]
        a, b = own(unit[1])
        for kind, by, part in ((1, 1, low), (2, -1, high)):
            behind = turn4(a, -by)
            block = view(unit, behind, b)
            remote(number + kind, block, block, along(unit[1], by, True)).wait_recv()
            block = view(unit, behind, b, part)
            go(remote(number + kind + 2, block, block, along(unit[1], by, True)))

    def second(unit):
        number = base[unit]
        a, b = own(unit[1])
        for kind, by, part in ((3, 1, low), (4, -1, high)):
            block = view(unit, turn4(a, 2), b, part)
            remote(number + kind, block, block, along(unit[1], by, True)).wait_recv()
        for kind, by in ((5, 1), (6, -1)):
            block = view(unit, whole, b)
            go(remote(number + kind, block, block, along(unit[1], by, False)))
        to_core(unit, 0, b)

    def second_forward(unit):
        number = base[unit]
        a, b = own(unit[1])
        for kind, by, part in ((5, 1, low), (6, -1, high)):
            behind = turn4(b, -by)
            block = view(unit, whole, behind)
            remote(number + kind, block, block, along(unit[1], by, False)).wait_recv()
            block = view(unit, whole, behind, part)
            go(remote(number + kind + 2, block, block, along(unit[1], by, False)))
        to_core(unit, 1, turn4(b, 1))
        to_core(unit, 2, turn4(b, -1))

    def complete(unit):
        number = base[unit]
        a, b = own(unit[1])
        for kind, by, part in ((7, 1, low), (8, -1, high)):
            block = view(unit, whole, turn4(b, 2), part)
            remote(number + kind, block, block, along(unit[1], by, False)).wait_recv()
        to_core(unit, 3, turn4(b, 2))

    def to_core(unit, part, b):
        j, h = unit
        where = (slice(None), slice(None), b) if h == 0 else (slice(None), b)
        core_copy[unit, part] = go(
            remote(
                base[unit] + 9 + part, got[j][0][h].at[where], got[j][1][h].at[where],
                place(x, y, z_hi, 1 - core),
            )
        )

    def from_core(unit):
        for part in range(4):
            core_copy[unit, part].wait_recv()

    def row_of(j, cc):
        return turn4(z_hi, -j) * 2 + (core if cc == 0 else 1 - core)

    def columns_of(j, core_of, h):
        start = (turn4(z_hi, -j) * 2 + core_of) * ROWS + h * BLOCK
        return pl.ds(pl.multiple_of(start, BLOCK), BLOCK)

    def depth_of(j, core_of, h):
        start = (ORDER[j, h] * 2 + lax.rem(core_of + core, 2)) * BLOCK
        return pl.ds(pl.multiple_of(start, BLOCK), BLOCK)

    def split_amplitudes():
        for j, h in PIECES:
            def one(core_of, carry, j=j, h=h):
                lanes = depth_of(j, core_of, h)
                a_high[:, lanes], a_low[:, lanes] = split(amp[:, columns_of(j, core_of, h)])
                return carry

            lax.fori_loop(0, 2, one, 0)

    def expand(j, cc, h):
        source = got[j][cc][h]
        row = row_of(j, cc) * 2 + h
        rows = pl.ds((ORDER[j, h] * 2 + cc) * BLOCK, BLOCK)

        def one(c, count):
            here = mask_ref[row, c]
            slot = jnp.minimum(count, SLOTS - 1)
            block = source[slot].reshape(BLOCK, BLOCK) * here.astype(F32)
            lanes = pl.ds(pl.multiple_of(c * BLOCK, BLOCK), BLOCK)
            w_high[rows, lanes], w_low[rows, lanes] = split(block)
            return count + here

        lax.fori_loop(0, BLOCKS, one, jnp.int32(0))

    def multiply(prod, first, count, n, add):
        rows = pl.ds(first * ROWS, count * ROWS)
        lanes = pl.ds(pl.multiple_of(n * 512, 512), 512)
        value = three_dots(a_high[:, rows], a_low[:, rows], w_high[rows, lanes], w_low[rows, lanes])
        if add:
            prod[:, lanes] += value
        else:
            prod[:, lanes] = value

    def multiply_all(prod, first, count, add):
        def one(n, carry):
            multiply(prod, first, count, n, add)
            return carry

        lax.fori_loop(0, WIDTH // 512, one, 0)

    xy = x * 4 + y

    def landing(sweep, c):
        return spread[sweep][c].at[p, :, pl.ds(pl.multiple_of(core * BLOCK, BLOCK), BLOCK)]

    def flip(sweep, c):
        for (j, h), (chunk, plane) in PIECES.items():
            if chunk != c:
                continue

            def one(other, carry, j=j, h=h, plane=plane):
                w = turn4(z_hi, j) * 2 + lax.rem(core + other, 2)
                lanes = pl.ds(pl.multiple_of(w * ROWS, ROWS), ROWS)
                block = prods[sweep][h * BLOCK:(h + 1) * BLOCK, lanes]
                turned_in[c][plane * 2 + other] = block.T.reshape(PLANE, SLAB, BLOCK)
                return carry

            lax.fori_loop(0, 2, one, 0)

    def send(sweep, c, other, step):
        number = sweep * 8 + c
        i = lax.rem(xy + step, PLANE)
        for (j, h), (chunk, plane) in PIECES.items():
            if chunk != c:
                continue
            w = turn4(z_hi, j) * 2 + lax.rem(core + other, 2)
            pltpu.make_async_remote_copy(
                src_ref=turned_in[c].at[plane * 2 + other, i], dst_ref=landing(sweep, c),
                send_sem=hop_out.at[number], recv_sem=hop_in.at[number],
                device_id={"pair": plane * PLANE + i, "virt": w}, device_id_type=MESH,
            ).start()

    def scatter(sweep, c):
        def one(step, carry):
            send(sweep, c, step // PLANE, lax.rem(step, PLANE))
            return carry

        if c:
            lax.fori_loop(0, PAIRS, one, 0)
            return
        lax.fori_loop(1, PAIRS, one, 0)
        pltpu.make_async_copy(
            turned_in[c].at[z_lo * 2, xy], landing(sweep, c), hop_in.at[sweep * 8]
        ).start()
        pltpu.make_async_remote_copy(
            src_ref=turned_in[c].at[2 - z_lo * 2, xy], dst_ref=landing(sweep, c),
            send_sem=hop_out.at[sweep * 8], recv_sem=hop_in.at[sweep * 8],
            device_id={"pair": (1 - z_lo) * PLANE + xy, "virt": v}, device_id_type=MESH,
        ).start()

    def give(sweep, c, beside=None):
        number = sweep * 8 + c
        pltpu.make_async_copy(spread[sweep][c], spread[sweep][c], hop_in.at[number]).wait()
        number += 4

        def one(step, carry):
            pair = lax.rem(p + lax.rem(step * 13, PAIRS), PAIRS)
            turned[c][pair] = spread[sweep][c][partner_ref[pair]]
            pltpu.make_async_remote_copy(
                src_ref=turned[c].at[pair], dst_ref=mirror[sweep][c].at[p],
                send_sem=hop_out.at[number], recv_sem=hop_in.at[number],
                device_id={"pair": pair}, device_id_type=MESH,
            ).start()
            if beside is not None:
                send(sweep, beside, step // PLANE, lax.rem(step, PLANE))
            return carry

        lax.fori_loop(1, PAIRS, one, 0)
        if beside is not None:
            send(sweep, beside, 0, 0)
        turned[c][p] = spread[sweep][c][partner_ref[p]]
        pltpu.make_async_copy(turned[c].at[p], mirror[sweep][c].at[p], hop_in.at[number]).start()

    def exchange(sweep, first, count):
        multiply(prods[sweep], first, count, z_hi, True)
        flip(sweep, 0)
        scatter(sweep, 0)
        for j in (1, 3):
            multiply(prods[sweep], first, count, turn4(z_hi, j), True)
        flip(sweep, 1)
        scatter(sweep, 1)
        flip(sweep, 2)
        multiply(prods[sweep], first, count, turn4(z_hi, 2), True)
        give(sweep, 0, 2)
        flip(sweep, 3)
        give(sweep, 1, 3)
        give(sweep, 2)
        give(sweep, 3)

    def combine(sweep, chunk):
        number = sweep * 8 + 4 + chunk
        pltpu.make_async_copy(mirror[sweep][chunk], mirror[sweep][chunk], hop_in.at[number]).wait()
        for (j, h), (c, plane) in PIECES.items():
            if c != chunk:
                continue

            def one(core_of, carry, j=j, h=h, plane=plane):
                lanes = columns_of(j, core_of, h)
                place = pl.ds(pl.multiple_of(core_of * BLOCK, BLOCK), BLOCK)
                other = mirror[sweep][chunk][plane * PLANE:(plane + 1) * PLANE, :, place]
                below = side[...] + virt_ref[:, lanes] + pair_ref[0]
                value = (ints[:, lanes] + prods[sweep][:, lanes] + other.reshape(ROWS, BLOCK)) / below
                if sweep == ITERS - 1:
                    out_ref[:, lanes] = value
                else:
                    depth = depth_of(j, core_of, h)
                    a_high[:, depth], a_low[:, depth] = split(value)
                return carry

            lax.fori_loop(0, 2, one, 0)

    def drain(sweep):
        sent = turned_in[0].at[pl.ds(0, 3)]
        pltpu.make_async_copy(sent, sent, hop_out.at[sweep * 8]).wait()
        sent = turned_in[0].at[0, pl.ds(0, PLANE - 1)]
        pltpu.make_async_copy(sent, sent, hop_out.at[sweep * 8]).wait()
        for c in range(CHUNKS):
            if c:
                pltpu.make_async_copy(turned_in[c], turned_in[c], hop_out.at[sweep * 8 + c]).wait()
            sent = turned[c].at[pl.ds(0, PAIRS - 1)]
            pltpu.make_async_copy(sent, sent, hop_out.at[sweep * 8 + 4 + c]).wait()

    near, far = units[:4], units[4:]
    for group in (near, far):
        for step in (from_z, first_forward, second):
            for unit in group:
                step(unit)
    own_energy = virt_ref[:, pl.ds(pl.multiple_of(v * ROWS, ROWS), ROWS)]
    side[...] = jnp.broadcast_to(own_energy, (BLOCK, ROWS)).T
    loads[-2].wait()
    split_amplitudes()
    for h in range(2):
        expand(0, 0, h)
    for unit in near:
        second_forward(unit)
    for h in range(2):
        core_copy[0, h].wait_recv()
        expand(0, 1, h)
    multiply_all(prods[0], 0, 2, False)
    for unit in far:
        second_forward(unit)
    for unit in units:
        complete(unit)
        expand(unit[0], 0, unit[1])
    for unit in units:
        from_core(unit)
        expand(unit[0], 1, unit[1])
        if unit != units[-1]:
            multiply_all(prods[0], ORDER[unit], 1, True)
    loads[-1].wait()
    exchange(0, ORDER[units[-1]], 1)
    combine(0, 0)
    combine(0, 1)
    multiply_all(prods[1], 0, 4, False)
    combine(0, 2)
    multiply_all(prods[1], 4, 2, True)
    combine(0, 3)
    drain(0)
    exchange(1, 6, 2)
    for c in range(CHUNKS):
        combine(1, c)
    drain(1)
    for copy in everything:
        copy.wait_send()


def per_device(amplitudes, integrals, operator, virt_energy, pair_energy, block_mask, partner):
    smem = pl.BlockSpec(memory_space=pltpu.SMEM)
    vmem = pl.BlockSpec(memory_space=pltpu.VMEM)
    hbm = pl.BlockSpec(memory_space=pl.ANY)
    slab = (PAIRS, SLAB, 2 * BLOCK)
    result = pl.pallas_call(
        kernel,
        out_shape=jax.ShapeDtypeStruct((ROWS, WIDTH), F32),
        in_specs=[smem] * 3 + [hbm] * 3 + [vmem],
        out_specs=vmem,
        scratch_shapes=[pltpu.VMEM((ROWS, WIDTH), F32)] * 2
        + [pltpu.VMEM((BLOCKS, BLOCK, BLOCK), F32)] * 2
        + [pltpu.VMEM((ROWS, BLOCK), F32)]
        + [pltpu.VMEM((ROWS, WIDTH), F32)] * 2
        + [pltpu.VMEM((ROWS, WIDTH), BF16)] * 2
        + [pltpu.VMEM((WIDTH, WIDTH), BF16)] * 2
        + [pltpu.VMEM((SLOTS, 4, 4, 8, BLOCK), F32)] * 16
        + [pltpu.VMEM((4, PLANE, SLAB, BLOCK), F32)] * 4
        + [pltpu.VMEM(slab, F32)] * 20
        + [
            pltpu.SemaphoreType.DMA((4,)),
            pltpu.SemaphoreType.DMA((6 * KINDS + 2,)),
            pltpu.SemaphoreType.DMA((6 * KINDS + 2,)),
            pltpu.SemaphoreType.DMA((16,)),
            pltpu.SemaphoreType.DMA((16,)),
            pltpu.SemaphoreType.REGULAR,
        ],
        compiler_params=pltpu.CompilerParams(
            collective_id=0, has_side_effects=True, vmem_limit_bytes=58 << 20
        ),
    )(
        partner, block_mask, pair_energy, amplitudes[0], integrals[0], operator, virt_energy[None],
    )
    return result[None]


def solution(mesh):
    return jax.shard_map(
        per_device,
        mesh=mesh,
        in_specs=(
            P("pair", "virt", None),
            P("pair", "virt", None),
            P("virt", None),
            P(),
            P("pair"),
            P(),
            P(),
        ),
        out_specs=P("pair", "virt", None),
        check_vma=False,
    )
```

```python
import jax
import jax.numpy as jnp
from jax import lax
from jax.experimental import pallas as pl
from jax.experimental.pallas import tpu as pltpu
from jax.sharding import PartitionSpec as P

ITERS = 2
MESH = pl.DeviceIdType.MESH
PAIRS, VIRTS = 32, 8
TOTAL = PAIRS * VIRTS
WIDTH, ROWS, BLOCK, BLOCKS, SLOTS = 2048, 256, 128, 16, 10
SLAB = 16
PLANE = PAIRS // 2
F32, BF16 = jnp.float32, jnp.bfloat16
NEAR, FAR, DIRECT = ((1, 1), (3, 0)), ((2, 0), (2, 1)), ((1, 0), (3, 1))
PARTS = 5
KINDS = 13
PIECES = {
    (0, 0): (0, 0), (0, 1): (0, 1), (1, 0): (1, 0), (3, 0): (1, 1),
    (1, 1): (2, 0), (3, 1): (2, 1), (2, 0): (3, 0), (2, 1): (3, 1),
}
CHUNKS = 4
ORDER = {piece: c * 2 + plane for piece, (c, plane) in PIECES.items()}


def split(value):
    high = value.astype(BF16)
    return high, (value - high.astype(F32)).astype(BF16)


def three_dots(a_high, a_low, b_high, b_low):
    def dot(a, b):
        return jnp.dot(a, b, preferred_element_type=F32)

    return dot(a_high, b_high) + (dot(a_high, b_low) + dot(a_low, b_high))


def kernel(
    partner_ref, mask_ref, pair_ref, amp_hbm, int_hbm, op_hbm, virt_ref,
    out_ref,
    amp, ints, op0, op1, side, prod0, prod1, a_high, a_low, w_high, w_low, *rest,
):
    got = [[[rest[(j * 2 + cc) * 2 + h] for h in range(2)] for cc in range(2)] for j in range(4)]
    rest = rest[16:]
    turned_in, spread, turned, mirror = (
        rest[0:4], (rest[4:8], rest[8:12]), rest[12:16], (rest[16:20], rest[20:24])
    )
    load_sem, gather_out, gather_in, hop_out, hop_in, ready = rest[24:]

    p, v = lax.axis_index("pair"), lax.axis_index("virt")
    z_lo, x, y = p // 16, lax.rem(p // 4, 4), lax.rem(p, 4)
    z_hi, core = v // 2, lax.rem(v, 2)
    op, prods = (op0, op1), (prod0, prod1)
    barrier = pltpu.get_barrier_semaphore()

    loads = [
        pltpu.make_async_copy(
            op_hbm.at[pl.ds(h * BLOCK, BLOCK), pl.ds(c * BLOCK, BLOCK)], op[h].at[c], load_sem.at[h]
        )
        for h in range(2) for c in range(BLOCKS)
    ] + [
        pltpu.make_async_copy(amp_hbm, amp, load_sem.at[2]),
        pltpu.make_async_copy(int_hbm, ints, load_sem.at[3]),
    ]
    for load in loads:
        load.start()

    def tell(semaphore, axis, mine, count):
        def one(step, carry):
            pl.semaphore_signal(
                semaphore, inc=1, device_id={axis: lax.rem(mine + step, count)}, device_id_type=MESH
            )
            return carry

        lax.fori_loop(1, count, one, 0)

    tell(barrier, "pair", p, PAIRS)
    tell(barrier, "virt", v, VIRTS)

    for h in range(2):
        pltpu.make_async_copy(op[h], op[h], load_sem.at[h]).wait()
        def find(c, carry, h=h):
            count, columns = carry
            here = mask_ref[v * 2 + h, c]
            columns = tuple(
                jnp.where((count == s) & (here > 0), c, column) for s, column in enumerate(columns)
            )
            return count + here, columns

        zero = jnp.int32(0)
        _, columns = lax.fori_loop(0, BLOCKS, find, (zero, (zero,) * SLOTS))
        for s in range(SLOTS):
            got[0][0][h][s] = op[h][columns[s]].reshape(4, 4, 8, BLOCK)

    pl.semaphore_wait(barrier, PAIRS + VIRTS - 2)
    tell(ready, "virt", v, VIRTS)
    pl.semaphore_wait(ready, VIRTS - 1)

    def place(xx, yy, zz, cc):
        return {"pair": (z_lo * 4 + xx) * 4 + yy, "virt": zz * 2 + cc}

    def remote(number, source, target, device):
        return pltpu.make_async_remote_copy(
            src_ref=source, dst_ref=target, send_sem=gather_out.at[number], recv_sem=gather_in.at[number],
            device_id=device, device_id_type=MESH,
        )

    everything = []

    def go(copy):
        copy.start()
        everything.append(copy)
        return copy

    def turn4(value, by):
        return lax.rem(value + (by + 4), 4)

    units = NEAR + FAR + DIRECT
    base = {u: i * KINDS for i, u in enumerate(units)}
    core_copy = {}
    for j, h in NEAR + FAR:
        block = got[0][0][h].at[:, x, y]
        go(remote(base[j, h], block, got[j][0][h].at[:, x, y], place(x, y, turn4(z_hi, j), core)))
    for h in range(2):
        core_copy[0, h] = go(
            remote(6 * KINDS + h, got[0][0][h], got[0][1][h], place(x, y, z_hi, 1 - core))
        )

    def direct(unit, part, first):
        j, h = unit
        slots = pl.ds(part * (SLOTS // PARTS), SLOTS // PARTS)
        z = turn4(z_hi, z_lo) if j == 1 else turn4(z_hi, z_lo - 1)
        device = {"pair": ((1 - z_lo) * 4 + x) * 4 + y, "virt": z * 2 + core}
        source = got[0 if first else j][0][h].at[slots]
        return remote(base[unit] + part, source, got[j][0][h].at[slots], device)

    def direct_start():
        for unit in DIRECT:
            @pl.when(z_lo == (1 if unit[0] == 1 else 0))
            def _():
                for part in range(PARTS):
                    direct(unit, part, True).start()

    def direct_pass(part):
        for unit in DIRECT:
            @pl.when(z_lo != (1 if unit[0] == 1 else 0))
            def _():
                direct(unit, part, False).wait_recv()
                direct(unit, part, False).start()

    def direct_end(unit):
        j, h = unit
        for part in range(PARTS):
            @pl.when(z_lo == (1 if j == 1 else 0))
            def _():
                direct(unit, part, False).wait_recv()

            slots = pl.ds(part * (SLOTS // PARTS), SLOTS // PARTS)
            core_copy[unit, part] = go(
                remote(
                    base[unit] + PARTS + part, got[j][0][h].at[slots], got[j][1][h].at[slots],
                    place(x, y, z_hi, 1 - core),
                )
            )

    def along(h, by, first):
        if (h == 0) == first:
            return place(turn4(x, by), y, z_hi, core)
        return place(x, turn4(y, by), z_hi, core)

    def view(unit, a, b, slots=slice(None)):
        j, h = unit
        i, k = (a, b) if h == 0 else (b, a)
        return got[j][0][h].at[slots, i, k]

    low, high = pl.ds(0, SLOTS // 2), pl.ds(SLOTS // 2, SLOTS // 2)
    whole = slice(None)

    def own(h):
        return (x, y) if h == 0 else (y, x)

    def from_z(unit):
        number = base[unit]
        a, b = own(unit[1])
        remote(number, view(unit, a, b), view(unit, a, b), place(x, y, z_hi, core)).wait_recv()
        for kind, by in ((1, 1), (2, -1)):
            go(remote(number + kind, view(unit, a, b), view(unit, a, b), along(unit[1], by, True)))

    def first_forward(unit):
        number = base[unit]
        a, b = own(unit[1])
        for kind, by, part in ((1, 1, low), (2, -1, high)):
            behind = turn4(a, -by)
            block = view(unit, behind, b)
            remote(number + kind, block, block, along(unit[1], by, True)).wait_recv()
            block = view(unit, behind, b, part)
            go(remote(number + kind + 2, block, block, along(unit[1], by, True)))

    def second(unit):
        number = base[unit]
        a, b = own(unit[1])
        for kind, by, part in ((3, 1, low), (4, -1, high)):
            block = view(unit, turn4(a, 2), b, part)
            remote(number + kind, block, block, along(unit[1], by, True)).wait_recv()
        for kind, by in ((5, 1), (6, -1)):
            block = view(unit, whole, b)
            go(remote(number + kind, block, block, along(unit[1], by, False)))
        to_core(unit, 0, b)

    def second_forward(unit):
        number = base[unit]
        a, b = own(unit[1])
        for kind, by, part in ((5, 1, low), (6, -1, high)):
            behind = turn4(b, -by)
            block = view(unit, whole, behind)
            remote(number + kind, block, block, along(unit[1], by, False)).wait_recv()
            block = view(unit, whole, behind, part)
            go(remote(number + kind + 2, block, block, along(unit[1], by, False)))
        to_core(unit, 1, turn4(b, 1))
        to_core(unit, 2, turn4(b, -1))

    def complete(unit):
        number = base[unit]
        a, b = own(unit[1])
        for kind, by, part in ((7, 1, low), (8, -1, high)):
            block = view(unit, whole, turn4(b, 2), part)
            remote(number + kind, block, block, along(unit[1], by, False)).wait_recv()
        to_core(unit, 3, turn4(b, 2))

    def to_core(unit, part, b):
        j, h = unit
        where = (slice(None), slice(None), b) if h == 0 else (slice(None), b)
        core_copy[unit, part] = go(
            remote(
                base[unit] + 9 + part, got[j][0][h].at[where], got[j][1][h].at[where],
                place(x, y, z_hi, 1 - core),
            )
        )

    def from_core(unit):
        for part in range(PARTS if unit in DIRECT else 4):
            core_copy[unit, part].wait_recv()

    def row_of(j, cc):
        return turn4(z_hi, -j) * 2 + (core if cc == 0 else 1 - core)

    def columns_of(j, core_of, h):
        start = (turn4(z_hi, -j) * 2 + core_of) * ROWS + h * BLOCK
        return pl.ds(pl.multiple_of(start, BLOCK), BLOCK)

    def depth_of(j, core_of, h):
        start = (ORDER[j, h] * 2 + lax.rem(core_of + core, 2)) * BLOCK
        return pl.ds(pl.multiple_of(start, BLOCK), BLOCK)

    def split_amplitudes():
        for j, h in PIECES:
            def one(core_of, carry, j=j, h=h):
                lanes = depth_of(j, core_of, h)
                a_high[:, lanes], a_low[:, lanes] = split(amp[:, columns_of(j, core_of, h)])
                return carry

            lax.fori_loop(0, 2, one, 0)

    def expand(j, cc, h):
        source = got[j][cc][h]
        row = row_of(j, cc) * 2 + h
        rows = pl.ds((ORDER[j, h] * 2 + cc) * BLOCK, BLOCK)

        def one(c, count):
            here = mask_ref[row, c]
            slot = jnp.minimum(count, SLOTS - 1)
            block = source[slot].reshape(BLOCK, BLOCK) * here.astype(F32)
            lanes = pl.ds(pl.multiple_of(c * BLOCK, BLOCK), BLOCK)
            w_high[rows, lanes], w_low[rows, lanes] = split(block)
            return count + here

        lax.fori_loop(0, BLOCKS, one, jnp.int32(0))

    def multiply(prod, first, count, n, add):
        rows = pl.ds(first * ROWS, count * ROWS)
        lanes = pl.ds(pl.multiple_of(n * 512, 512), 512)
        value = three_dots(a_high[:, rows], a_low[:, rows], w_high[rows, lanes], w_low[rows, lanes])
        if add:
            prod[:, lanes] += value
        else:
            prod[:, lanes] = value

    def multiply_all(prod, first, count, add):
        def one(n, carry):
            multiply(prod, first, count, n, add)
            return carry

        lax.fori_loop(0, WIDTH // 512, one, 0)

    xy = x * 4 + y

    def landing(sweep, c):
        return spread[sweep][c].at[p, :, pl.ds(pl.multiple_of(core * BLOCK, BLOCK), BLOCK)]

    def flip(sweep, c):
        for (j, h), (chunk, plane) in PIECES.items():
            if chunk != c:
                continue

            def one(other, carry, j=j, h=h, plane=plane):
                w = turn4(z_hi, j) * 2 + lax.rem(core + other, 2)
                lanes = pl.ds(pl.multiple_of(w * ROWS, ROWS), ROWS)
                block = prods[sweep][h * BLOCK:(h + 1) * BLOCK, lanes]
                turned_in[c][plane * 2 + other] = block.T.reshape(PLANE, SLAB, BLOCK)
                return carry

            lax.fori_loop(0, 2, one, 0)

    def send(sweep, c, other, step):
        number = sweep * 8 + c
        i = lax.rem(xy + step, PLANE)
        for (j, h), (chunk, plane) in PIECES.items():
            if chunk != c:
                continue
            w = turn4(z_hi, j) * 2 + lax.rem(core + other, 2)
            pltpu.make_async_remote_copy(
                src_ref=turned_in[c].at[plane * 2 + other, i], dst_ref=landing(sweep, c),
                send_sem=hop_out.at[number], recv_sem=hop_in.at[number],
                device_id={"pair": plane * PLANE + i, "virt": w}, device_id_type=MESH,
            ).start()

    def scatter(sweep, c):
        def one(step, carry):
            send(sweep, c, step // PLANE, lax.rem(step, PLANE))
            return carry

        if c:
            lax.fori_loop(0, PAIRS, one, 0)
            return
        lax.fori_loop(1, PAIRS, one, 0)
        pltpu.make_async_copy(
            turned_in[c].at[z_lo * 2, xy], landing(sweep, c), hop_in.at[sweep * 8]
        ).start()
        pltpu.make_async_remote_copy(
            src_ref=turned_in[c].at[2 - z_lo * 2, xy], dst_ref=landing(sweep, c),
            send_sem=hop_out.at[sweep * 8], recv_sem=hop_in.at[sweep * 8],
            device_id={"pair": (1 - z_lo) * PLANE + xy, "virt": v}, device_id_type=MESH,
        ).start()

    def give(sweep, c, beside=None):
        number = sweep * 8 + c
        pltpu.make_async_copy(spread[sweep][c], spread[sweep][c], hop_in.at[number]).wait()
        number += 4

        def one(step, carry):
            pair = lax.rem(p + lax.rem(step * 13, PAIRS), PAIRS)
            turned[c][pair] = spread[sweep][c][partner_ref[pair]]
            pltpu.make_async_remote_copy(
                src_ref=turned[c].at[pair], dst_ref=mirror[sweep][c].at[p],
                send_sem=hop_out.at[number], recv_sem=hop_in.at[number],
                device_id={"pair": pair}, device_id_type=MESH,
            ).start()
            if beside is not None:
                send(sweep, beside, step // PLANE, lax.rem(step, PLANE))
            return carry

        lax.fori_loop(1, PAIRS, one, 0)
        if beside is not None:
            send(sweep, beside, 0, 0)
        turned[c][p] = spread[sweep][c][partner_ref[p]]
        pltpu.make_async_copy(turned[c].at[p], mirror[sweep][c].at[p], hop_in.at[number]).start()

    def exchange(sweep, first, count):
        multiply(prods[sweep], first, count, z_hi, True)
        flip(sweep, 0)
        scatter(sweep, 0)
        for j in (1, 3):
            multiply(prods[sweep], first, count, turn4(z_hi, j), True)
        flip(sweep, 1)
        scatter(sweep, 1)
        flip(sweep, 2)
        multiply(prods[sweep], first, count, turn4(z_hi, 2), True)
        give(sweep, 0, 2)
        flip(sweep, 3)
        give(sweep, 1, 3)
        give(sweep, 2)
        give(sweep, 3)

    def combine(sweep, chunk):
        number = sweep * 8 + 4 + chunk
        pltpu.make_async_copy(mirror[sweep][chunk], mirror[sweep][chunk], hop_in.at[number]).wait()
        for (j, h), (c, plane) in PIECES.items():
            if c != chunk:
                continue

            def one(core_of, carry, j=j, h=h, plane=plane):
                lanes = columns_of(j, core_of, h)
                place = pl.ds(pl.multiple_of(core_of * BLOCK, BLOCK), BLOCK)
                other = mirror[sweep][chunk][plane * PLANE:(plane + 1) * PLANE, :, place]
                below = side[...] + virt_ref[:, lanes] + pair_ref[0]
                value = (ints[:, lanes] + prods[sweep][:, lanes] + other.reshape(ROWS, BLOCK)) / below
                if sweep == ITERS - 1:
                    out_ref[:, lanes] = value
                else:
                    depth = depth_of(j, core_of, h)
                    a_high[:, depth], a_low[:, depth] = split(value)
                return carry

            lax.fori_loop(0, 2, one, 0)

    def drain(sweep):
        sent = turned_in[0].at[pl.ds(0, 3)]
        pltpu.make_async_copy(sent, sent, hop_out.at[sweep * 8]).wait()
        sent = turned_in[0].at[0, pl.ds(0, PLANE - 1)]
        pltpu.make_async_copy(sent, sent, hop_out.at[sweep * 8]).wait()
        for c in range(CHUNKS):
            if c:
                pltpu.make_async_copy(turned_in[c], turned_in[c], hop_out.at[sweep * 8 + c]).wait()
            sent = turned[c].at[pl.ds(0, PAIRS - 1)]
            pltpu.make_async_copy(sent, sent, hop_out.at[sweep * 8 + 4 + c]).wait()

    for unit in NEAR + FAR:
        from_z(unit)
    direct_start()
    for unit in NEAR + FAR:
        first_forward(unit)
    for unit in NEAR + FAR:
        second(unit)
    direct_pass(0)
    direct_pass(1)
    own_energy = virt_ref[:, pl.ds(pl.multiple_of(v * ROWS, ROWS), ROWS)]
    side[...] = jnp.broadcast_to(own_energy, (BLOCK, ROWS)).T
    loads[-2].wait()
    split_amplitudes()
    for h in range(2):
        expand(0, 0, h)
    direct_pass(2)
    for unit in NEAR:
        second_forward(unit)
    for h in range(2):
        core_copy[0, h].wait_recv()
        expand(0, 1, h)
    direct_pass(3)
    for unit in FAR:
        second_forward(unit)
    direct_pass(4)
    multiply_all(prods[0], 0, 2, False)

    def use(unit):
        from_core(unit)
        expand(unit[0], 1, unit[1])
        if unit != FAR[1]:
            multiply_all(prods[0], ORDER[unit], 1, True)

    for unit in NEAR:
        complete(unit)
        expand(unit[0], 0, unit[1])
    for unit in DIRECT:
        direct_end(unit)
        expand(unit[0], 0, unit[1])
    for unit in NEAR:
        use(unit)
    for unit in FAR:
        complete(unit)
        expand(unit[0], 0, unit[1])
    for unit in DIRECT + FAR:
        use(unit)
    loads[-1].wait()
    exchange(0, ORDER[FAR[1]], 1)
    combine(0, 0)
    combine(0, 1)
    multiply_all(prods[1], 0, 4, False)
    combine(0, 2)
    multiply_all(prods[1], 4, 2, True)
    combine(0, 3)
    drain(0)
    exchange(1, 6, 2)
    for c in range(CHUNKS):
        combine(1, c)
    drain(1)
    for copy in everything:
        copy.wait_send()
    for unit in DIRECT:
        for part in range(PARTS):
            direct(unit, part, False).wait_send()


def per_device(amplitudes, integrals, operator, virt_energy, pair_energy, block_mask, partner):
    smem = pl.BlockSpec(memory_space=pltpu.SMEM)
    vmem = pl.BlockSpec(memory_space=pltpu.VMEM)
    hbm = pl.BlockSpec(memory_space=pl.ANY)
    slab = (PAIRS, SLAB, 2 * BLOCK)
    result = pl.pallas_call(
        kernel,
        out_shape=jax.ShapeDtypeStruct((ROWS, WIDTH), F32),
        in_specs=[smem] * 3 + [hbm] * 3 + [vmem],
        out_specs=vmem,
        scratch_shapes=[pltpu.VMEM((ROWS, WIDTH), F32)] * 2
        + [pltpu.VMEM((BLOCKS, BLOCK, BLOCK), F32)] * 2
        + [pltpu.VMEM((ROWS, BLOCK), F32)]
        + [pltpu.VMEM((ROWS, WIDTH), F32)] * 2
        + [pltpu.VMEM((ROWS, WIDTH), BF16)] * 2
        + [pltpu.VMEM((WIDTH, WIDTH), BF16)] * 2
        + [pltpu.VMEM((SLOTS, 4, 4, 8, BLOCK), F32)] * 16
        + [pltpu.VMEM((4, PLANE, SLAB, BLOCK), F32)] * 4
        + [pltpu.VMEM(slab, F32)] * 20
        + [
            pltpu.SemaphoreType.DMA((4,)),
            pltpu.SemaphoreType.DMA((6 * KINDS + 2,)),
            pltpu.SemaphoreType.DMA((6 * KINDS + 2,)),
            pltpu.SemaphoreType.DMA((16,)),
            pltpu.SemaphoreType.DMA((16,)),
            pltpu.SemaphoreType.REGULAR,
        ],
        compiler_params=pltpu.CompilerParams(
            collective_id=0, has_side_effects=True, vmem_limit_bytes=58 << 20
        ),
    )(
        partner, block_mask, pair_energy, amplitudes[0], integrals[0], operator, virt_energy[None],
    )
    return result[None]


def solution(mesh):
    return jax.shard_map(
        per_device,
        mesh=mesh,
        in_specs=(
            P("pair", "virt", None),
            P("pair", "virt", None),
            P("virt", None),
            P(),
            P("pair"),
            P(),
            P(),
        ),
        out_specs=P("pair", "virt", None),
        check_vma=False,
    )
```

```python
import jax
import jax.numpy as jnp
from jax import lax
from jax.experimental import pallas as pl
from jax.experimental.pallas import tpu as pltpu
from jax.sharding import PartitionSpec as P

ITERS = 2
MESH = pl.DeviceIdType.MESH
PAIRS, VIRTS = 32, 8
TOTAL = PAIRS * VIRTS
WIDTH, ROWS, BLOCK, BLOCKS, SLOTS = 2048, 256, 128, 16, 10
SLAB = 16
PLANE = PAIRS // 2
F32, BF16 = jnp.float32, jnp.bfloat16
NEAR, FAR, DIRECT = ((1, 1), (3, 0)), ((2, 0), (2, 1)), ((1, 0), (3, 1))
PARTS = 5
KINDS = 13
PIECES = {
    (0, 0): (0, 0), (0, 1): (0, 1), (1, 0): (1, 0), (3, 0): (1, 1),
    (1, 1): (2, 0), (3, 1): (2, 1), (2, 0): (3, 0), (2, 1): (3, 1),
}
CHUNKS = 4
ORDER = {piece: c * 2 + plane for piece, (c, plane) in PIECES.items()}


def split(value):
    high = value.astype(BF16)
    return high, (value - high.astype(F32)).astype(BF16)


def three_dots(a_high, a_low, b_high, b_low):
    def dot(a, b):
        return jnp.dot(a, b, preferred_element_type=F32)

    return dot(a_high, b_high) + (dot(a_high, b_low) + dot(a_low, b_high))


def kernel(
    partner_ref, mask_ref, pair_ref, amp_hbm, int_hbm, op_hbm, virt_ref,
    out_ref,
    amp, ints, op0, op1, side, prod0, prod1, a_high, a_low, w_high, w_low, *rest,
):
    got = [[[rest[(j * 2 + cc) * 2 + h] for h in range(2)] for cc in range(2)] for j in range(4)]
    rest = rest[16:]
    turned_in, spread, turned, mirror = (
        rest[0:4], (rest[4:8], rest[8:12]), rest[12:16], (rest[16:20], rest[20:24])
    )
    load_sem, gather_out, gather_in, hop_out, hop_in, ready = rest[24:]

    p, v = lax.axis_index("pair"), lax.axis_index("virt")
    z_lo, x, y = p // 16, lax.rem(p // 4, 4), lax.rem(p, 4)
    z_hi, core = v // 2, lax.rem(v, 2)
    op, prods = (op0, op1), (prod0, prod1)
    barrier = pltpu.get_barrier_semaphore()

    loads = [
        pltpu.make_async_copy(
            op_hbm.at[pl.ds(h * BLOCK, BLOCK), pl.ds(c * BLOCK, BLOCK)], op[h].at[c], load_sem.at[h]
        )
        for h in range(2) for c in range(BLOCKS)
    ] + [
        pltpu.make_async_copy(amp_hbm, amp, load_sem.at[2]),
        pltpu.make_async_copy(int_hbm, ints, load_sem.at[3]),
    ]
    for load in loads:
        load.start()

    def tell(semaphore, axis, mine, count):
        def one(step, carry):
            pl.semaphore_signal(
                semaphore, inc=1, device_id={axis: lax.rem(mine + step, count)}, device_id_type=MESH
            )
            return carry

        lax.fori_loop(1, count, one, 0)

    tell(barrier, "pair", p, PAIRS)
    tell(barrier, "virt", v, VIRTS)

    for h in range(2):
        pltpu.make_async_copy(op[h], op[h], load_sem.at[h]).wait()
        def find(c, carry, h=h):
            count, columns = carry
            here = mask_ref[v * 2 + h, c]
            columns = tuple(
                jnp.where((count == s) & (here > 0), c, column) for s, column in enumerate(columns)
            )
            return count + here, columns

        zero = jnp.int32(0)
        _, columns = lax.fori_loop(0, BLOCKS, find, (zero, (zero,) * SLOTS))
        for s in range(SLOTS):
            got[0][0][h][s] = op[h][columns[s]].reshape(4, 4, 8, BLOCK)

    pl.semaphore_wait(barrier, PAIRS + VIRTS - 2)
    tell(ready, "virt", v, VIRTS)
    pl.semaphore_wait(ready, VIRTS - 1)

    def place(xx, yy, zz, cc):
        return {"pair": (z_lo * 4 + xx) * 4 + yy, "virt": zz * 2 + cc}

    def remote(number, source, target, device):
        return pltpu.make_async_remote_copy(
            src_ref=source, dst_ref=target, send_sem=gather_out.at[number], recv_sem=gather_in.at[number],
            device_id=device, device_id_type=MESH,
        )

    everything = []

    def go(copy):
        copy.start()
        everything.append(copy)
        return copy

    def turn4(value, by):
        return lax.rem(value + (by + 4), 4)

    units = NEAR + FAR + DIRECT
    base = {u: i * KINDS for i, u in enumerate(units)}
    core_copy = {}
    for j, h in NEAR + FAR:
        block = got[0][0][h].at[:, x, y]
        go(remote(base[j, h], block, got[j][0][h].at[:, x, y], place(x, y, turn4(z_hi, j), core)))
    for h in range(2):
        core_copy[0, h] = go(
            remote(6 * KINDS + h, got[0][0][h], got[0][1][h], place(x, y, z_hi, 1 - core))
        )

    def direct(unit, part, first):
        j, h = unit
        slots = pl.ds(part * (SLOTS // PARTS), SLOTS // PARTS)
        z = turn4(z_hi, z_lo) if j == 1 else turn4(z_hi, z_lo - 1)
        device = {"pair": ((1 - z_lo) * 4 + x) * 4 + y, "virt": z * 2 + core}
        source = got[0 if first else j][0][h].at[slots]
        return remote(base[unit] + part, source, got[j][0][h].at[slots], device)

    def direct_start():
        for unit in DIRECT:
            @pl.when(z_lo == (1 if unit[0] == 1 else 0))
            def _():
                for part in range(PARTS):
                    direct(unit, part, True).start()

    def direct_pass(part):
        for unit in DIRECT:
            @pl.when(z_lo != (1 if unit[0] == 1 else 0))
            def _():
                direct(unit, part, False).wait_recv()
                direct(unit, part, False).start()

    def direct_end(unit):
        j, h = unit
        for part in range(PARTS):
            @pl.when(z_lo == (1 if j == 1 else 0))
            def _():
                direct(unit, part, False).wait_recv()

            slots = pl.ds(part * (SLOTS // PARTS), SLOTS // PARTS)
            core_copy[unit, part] = go(
                remote(
                    base[unit] + PARTS + part, got[j][0][h].at[slots], got[j][1][h].at[slots],
                    place(x, y, z_hi, 1 - core),
                )
            )

    def along(h, by, first):
        if (h == 0) == first:
            return place(turn4(x, by), y, z_hi, core)
        return place(x, turn4(y, by), z_hi, core)

    def view(unit, a, b, slots=slice(None)):
        j, h = unit
        i, k = (a, b) if h == 0 else (b, a)
        return got[j][0][h].at[slots, i, k]

    low, high = pl.ds(0, SLOTS // 2), pl.ds(SLOTS // 2, SLOTS // 2)
    whole = slice(None)

    def own(h):
        return (x, y) if h == 0 else (y, x)

    def from_z(unit):
        number = base[unit]
        a, b = own(unit[1])
        remote(number, view(unit, a, b), view(unit, a, b), place(x, y, z_hi, core)).wait_recv()
        for kind, by in ((1, 1), (2, -1)):
            go(remote(number + kind, view(unit, a, b), view(unit, a, b), along(unit[1], by, True)))

    def first_forward(unit):
        number = base[unit]
        a, b = own(unit[1])
        for kind, by, part in ((1, 1, low), (2, -1, high)):
            behind = turn4(a, -by)
            block = view(unit, behind, b)
            remote(number + kind, block, block, along(unit[1], by, True)).wait_recv()
            block = view(unit, behind, b, part)
            go(remote(number + kind + 2, block, block, along(unit[1], by, True)))

    def second(unit):
        number = base[unit]
        a, b = own(unit[1])
        for kind, by, part in ((3, 1, low), (4, -1, high)):
            block = view(unit, turn4(a, 2), b, part)
            remote(number + kind, block, block, along(unit[1], by, True)).wait_recv()
        for kind, by in ((5, 1), (6, -1)):
            block = view(unit, whole, b)
            go(remote(number + kind, block, block, along(unit[1], by, False)))
        to_core(unit, 0, b)

    def second_forward(unit):
        number = base[unit]
        a, b = own(unit[1])
        for kind, by, part in ((5, 1, low), (6, -1, high)):
            behind = turn4(b, -by)
            block = view(unit, whole, behind)
            remote(number + kind, block, block, along(unit[1], by, False)).wait_recv()
            block = view(unit, whole, behind, part)
            go(remote(number + kind + 2, block, block, along(unit[1], by, False)))
        to_core(unit, 1, turn4(b, 1))
        to_core(unit, 2, turn4(b, -1))

    def complete(unit):
        number = base[unit]
        a, b = own(unit[1])
        for kind, by, part in ((7, 1, low), (8, -1, high)):
            block = view(unit, whole, turn4(b, 2), part)
            remote(number + kind, block, block, along(unit[1], by, False)).wait_recv()
        to_core(unit, 3, turn4(b, 2))

    def to_core(unit, part, b):
        j, h = unit
        where = (slice(None), slice(None), b) if h == 0 else (slice(None), b)
        core_copy[unit, part] = go(
            remote(
                base[unit] + 9 + part, got[j][0][h].at[where], got[j][1][h].at[where],
                place(x, y, z_hi, 1 - core),
            )
        )

    def from_core(unit):
        for part in range(PARTS if unit in DIRECT else 4):
            core_copy[unit, part].wait_recv()

    def row_of(j, cc):
        return turn4(z_hi, -j) * 2 + (core if cc == 0 else 1 - core)

    def columns_of(j, core_of, h):
        start = (turn4(z_hi, -j) * 2 + core_of) * ROWS + h * BLOCK
        return pl.ds(pl.multiple_of(start, BLOCK), BLOCK)

    def depth_of(j, core_of, h):
        start = (ORDER[j, h] * 2 + lax.rem(core_of + core, 2)) * BLOCK
        return pl.ds(pl.multiple_of(start, BLOCK), BLOCK)

    def split_amplitudes():
        for j, h in PIECES:
            def one(core_of, carry, j=j, h=h):
                lanes = depth_of(j, core_of, h)
                a_high[:, lanes], a_low[:, lanes] = split(amp[:, columns_of(j, core_of, h)])
                return carry

            lax.fori_loop(0, 2, one, 0)

    def expand(j, cc, h):
        source = got[j][cc][h]
        row = row_of(j, cc) * 2 + h
        rows = pl.ds((ORDER[j, h] * 2 + cc) * BLOCK, BLOCK)

        def one(c, count):
            here = mask_ref[row, c]
            slot = jnp.minimum(count, SLOTS - 1)
            block = source[slot].reshape(BLOCK, BLOCK) * here.astype(F32)
            lanes = pl.ds(pl.multiple_of(c * BLOCK, BLOCK), BLOCK)
            w_high[rows, lanes], w_low[rows, lanes] = split(block)
            return count + here

        lax.fori_loop(0, BLOCKS, one, jnp.int32(0))

    def multiply(prod, first, count, n, add):
        rows = pl.ds(first * ROWS, count * ROWS)
        lanes = pl.ds(pl.multiple_of(n * 512, 512), 512)
        value = three_dots(a_high[:, rows], a_low[:, rows], w_high[rows, lanes], w_low[rows, lanes])
        if add:
            prod[:, lanes] += value
        else:
            prod[:, lanes] = value

    def multiply_all(prod, first, count, add):
        def one(n, carry):
            multiply(prod, first, count, n, add)
            return carry

        lax.fori_loop(0, WIDTH // 512, one, 0)

    xy = x * 4 + y

    def landing(sweep, c):
        return spread[sweep][c].at[p, :, pl.ds(pl.multiple_of(core * BLOCK, BLOCK), BLOCK)]

    def flip(sweep, c):
        for (j, h), (chunk, plane) in PIECES.items():
            if chunk != c:
                continue

            def one(other, carry, j=j, h=h, plane=plane):
                w = turn4(z_hi, j) * 2 + lax.rem(core + other, 2)
                lanes = pl.ds(pl.multiple_of(w * ROWS, ROWS), ROWS)
                block = prods[sweep][h * BLOCK:(h + 1) * BLOCK, lanes]
                turned_in[c][plane * 2 + other] = block.T.reshape(PLANE, SLAB, BLOCK)
                return carry

            lax.fori_loop(0, 2, one, 0)

    def send(sweep, c, other, step):
        number = sweep * 8 + c
        i = lax.rem(xy + step, PLANE)
        for (j, h), (chunk, plane) in PIECES.items():
            if chunk != c:
                continue
            w = turn4(z_hi, j) * 2 + lax.rem(core + other, 2)
            pltpu.make_async_remote_copy(
                src_ref=turned_in[c].at[plane * 2 + other, i], dst_ref=landing(sweep, c),
                send_sem=hop_out.at[number], recv_sem=hop_in.at[number],
                device_id={"pair": plane * PLANE + i, "virt": w}, device_id_type=MESH,
            ).start()

    def scatter(sweep, c):
        def one(step, carry):
            send(sweep, c, step // PLANE, lax.rem(step, PLANE))
            return carry

        if c:
            lax.fori_loop(0, PAIRS, one, 0)
            return
        lax.fori_loop(1, PAIRS, one, 0)
        pltpu.make_async_copy(
            turned_in[c].at[z_lo * 2, xy], landing(sweep, c), hop_in.at[sweep * 8]
        ).start()
        pltpu.make_async_remote_copy(
            src_ref=turned_in[c].at[2 - z_lo * 2, xy], dst_ref=landing(sweep, c),
            send_sem=hop_out.at[sweep * 8], recv_sem=hop_in.at[sweep * 8],
            device_id={"pair": (1 - z_lo) * PLANE + xy, "virt": v}, device_id_type=MESH,
        ).start()

    def give(sweep, c, beside=None):
        number = sweep * 8 + c
        pltpu.make_async_copy(spread[sweep][c], spread[sweep][c], hop_in.at[number]).wait()
        number += 4

        def one(step, carry):
            pair = lax.rem(p + lax.rem(step * 13, PAIRS), PAIRS)
            turned[c][pair] = spread[sweep][c][partner_ref[pair]]
            pltpu.make_async_remote_copy(
                src_ref=turned[c].at[pair], dst_ref=mirror[sweep][c].at[p],
                send_sem=hop_out.at[number], recv_sem=hop_in.at[number],
                device_id={"pair": pair}, device_id_type=MESH,
            ).start()
            if beside is not None:
                send(sweep, beside, step // PLANE, lax.rem(step, PLANE))
            return carry

        lax.fori_loop(1, PAIRS, one, 0)
        if beside is not None:
            send(sweep, beside, 0, 0)
        turned[c][p] = spread[sweep][c][partner_ref[p]]
        pltpu.make_async_copy(turned[c].at[p], mirror[sweep][c].at[p], hop_in.at[number]).start()

    def combine(sweep, chunk):
        number = sweep * 8 + 4 + chunk
        pltpu.make_async_copy(mirror[sweep][chunk], mirror[sweep][chunk], hop_in.at[number]).wait()
        for (j, h), (c, plane) in PIECES.items():
            if c != chunk:
                continue

            def one(core_of, carry, j=j, h=h, plane=plane):
                lanes = columns_of(j, core_of, h)
                place = pl.ds(pl.multiple_of(core_of * BLOCK, BLOCK), BLOCK)
                other = mirror[sweep][chunk][plane * PLANE:(plane + 1) * PLANE, :, place]
                below = side[...] + virt_ref[:, lanes] + pair_ref[0]
                value = (ints[:, lanes] + prods[sweep][:, lanes] + other.reshape(ROWS, BLOCK)) / below
                if sweep == ITERS - 1:
                    out_ref[:, lanes] = value
                else:
                    depth = depth_of(j, core_of, h)
                    a_high[:, depth], a_low[:, depth] = split(value)
                return carry

            lax.fori_loop(0, 2, one, 0)

    def exchange(sweep, first, count):
        multiply(prods[sweep], first, count, z_hi, True)
        flip(sweep, 0)
        scatter(sweep, 0)
        for j in (1, 3):
            multiply(prods[sweep], first, count, turn4(z_hi, j), True)
        flip(sweep, 1)
        scatter(sweep, 1)
        flip(sweep, 2)
        multiply(prods[sweep], first, count, turn4(z_hi, 2), True)
        give(sweep, 0, 2)
        flip(sweep, 3)
        give(sweep, 1, 3)
        give(sweep, 2)
        combine(sweep, 0)
        combine(sweep, 1)
        if sweep == 0:
            multiply_all(prods[1], 0, 4, False)
        give(sweep, 3)

    def drain(sweep):
        sent = turned_in[0].at[pl.ds(0, 3)]
        pltpu.make_async_copy(sent, sent, hop_out.at[sweep * 8]).wait()
        sent = turned_in[0].at[0, pl.ds(0, PLANE - 1)]
        pltpu.make_async_copy(sent, sent, hop_out.at[sweep * 8]).wait()
        for c in range(CHUNKS):
            if c:
                pltpu.make_async_copy(turned_in[c], turned_in[c], hop_out.at[sweep * 8 + c]).wait()
            sent = turned[c].at[pl.ds(0, PAIRS - 1)]
            pltpu.make_async_copy(sent, sent, hop_out.at[sweep * 8 + 4 + c]).wait()

    for unit in NEAR + FAR:
        from_z(unit)
    direct_start()
    for unit in NEAR + FAR:
        first_forward(unit)
    for unit in NEAR + FAR:
        second(unit)
    direct_pass(0)
    direct_pass(1)
    own_energy = virt_ref[:, pl.ds(pl.multiple_of(v * ROWS, ROWS), ROWS)]
    side[...] = jnp.broadcast_to(own_energy, (BLOCK, ROWS)).T
    loads[-2].wait()
    split_amplitudes()
    for h in range(2):
        expand(0, 0, h)
    direct_pass(2)
    for unit in NEAR:
        second_forward(unit)
    for h in range(2):
        core_copy[0, h].wait_recv()
        expand(0, 1, h)
    direct_pass(3)
    for unit in FAR:
        second_forward(unit)
    direct_pass(4)
    multiply_all(prods[0], 0, 2, False)

    def use(unit):
        from_core(unit)
        expand(unit[0], 1, unit[1])
        if unit != FAR[1]:
            multiply_all(prods[0], ORDER[unit], 1, True)

    for unit in NEAR:
        complete(unit)
        expand(unit[0], 0, unit[1])
    for unit in DIRECT:
        direct_end(unit)
        expand(unit[0], 0, unit[1])
    for unit in NEAR:
        use(unit)
    for unit in FAR:
        complete(unit)
        expand(unit[0], 0, unit[1])
    for unit in DIRECT + FAR:
        use(unit)
    loads[-1].wait()
    exchange(0, ORDER[FAR[1]], 1)
    combine(0, 2)
    multiply_all(prods[1], 4, 2, True)
    combine(0, 3)
    drain(0)
    exchange(1, 6, 2)
    for c in (2, 3):
        combine(1, c)
    drain(1)
    for copy in everything:
        copy.wait_send()
    for unit in DIRECT:
        for part in range(PARTS):
            direct(unit, part, False).wait_send()


def per_device(amplitudes, integrals, operator, virt_energy, pair_energy, block_mask, partner):
    smem = pl.BlockSpec(memory_space=pltpu.SMEM)
    vmem = pl.BlockSpec(memory_space=pltpu.VMEM)
    hbm = pl.BlockSpec(memory_space=pl.ANY)
    slab = (PAIRS, SLAB, 2 * BLOCK)
    result = pl.pallas_call(
        kernel,
        out_shape=jax.ShapeDtypeStruct((ROWS, WIDTH), F32),
        in_specs=[smem] * 3 + [hbm] * 3 + [vmem],
        out_specs=vmem,
        scratch_shapes=[pltpu.VMEM((ROWS, WIDTH), F32)] * 2
        + [pltpu.VMEM((BLOCKS, BLOCK, BLOCK), F32)] * 2
        + [pltpu.VMEM((ROWS, BLOCK), F32)]
        + [pltpu.VMEM((ROWS, WIDTH), F32)] * 2
        + [pltpu.VMEM((ROWS, WIDTH), BF16)] * 2
        + [pltpu.VMEM((WIDTH, WIDTH), BF16)] * 2
        + [pltpu.VMEM((SLOTS, 4, 4, 8, BLOCK), F32)] * 16
        + [pltpu.VMEM((4, PLANE, SLAB, BLOCK), F32)] * 4
        + [pltpu.VMEM(slab, F32)] * 20
        + [
            pltpu.SemaphoreType.DMA((4,)),
            pltpu.SemaphoreType.DMA((6 * KINDS + 2,)),
            pltpu.SemaphoreType.DMA((6 * KINDS + 2,)),
            pltpu.SemaphoreType.DMA((16,)),
            pltpu.SemaphoreType.DMA((16,)),
            pltpu.SemaphoreType.REGULAR,
        ],
        compiler_params=pltpu.CompilerParams(
            collective_id=0, has_side_effects=True, vmem_limit_bytes=58 << 20
        ),
    )(
        partner, block_mask, pair_energy, amplitudes[0], integrals[0], operator, virt_energy[None],
    )
    return result[None]


def solution(mesh):
    return jax.shard_map(
        per_device,
        mesh=mesh,
        in_specs=(
            P("pair", "virt", None),
            P("pair", "virt", None),
            P("virt", None),
            P(),
            P("pair"),
            P(),
            P(),
        ),
        out_specs=P("pair", "virt", None),
        check_vma=False,
    )
```
